32 devices in a mesh: blk: 8 (over z, y), col: 4 (over x, core).
Axes of the slice: x: 2, y: 2, z: 4, core: 2. Of those that a mesh axis runs over, the one named last changes fastest.
Arguments:
- start_panel: float32 [128, 16384], P('col', 'blk'), may hold values from -6 to 6
- tile_values: float32 [192, 128, 128], P('blk'), may hold values from -0.3125 to 0.3125
- tile_rows: int32 [192], P('blk'), may hold values from 0 to 127, as said below
- tile_cols: int32 [192], P('blk'), may hold values from 0 to 127, as said below
- tile_counts: int32 [8], P('blk'), may hold values from 5 to 24, as said below
Outputs:
- ortho_panel: float32 [128, 16384], P('col', 'blk')
- gram_factor: float32 [128, 128], replicated
The draws below stay inside these ranges and needn't reach their ends.
Inputs may be any that keep to these rules, and one draw needn't show every extreme that they name: `tile_rows`: slot s has a row block among those of blk index s // 24, that is s // 24 * 16 up to s // 24 * 16 + 15. `tile_cols`: slot s has a column block among those of blk indices s // 24 + o for o from -2 to 2, taken modulo the number of blk indices; slot j of each blk index with j < 5 takes o = j - 2. `tile_counts`: some blk index has all 24 slots live; every blk index has 5 or more.
All inputs are finite; a program needn't handle non-finite values.
Results may differ from the reference program's by a relative error of at most 0.0003.
Values sent between devices are 32-bit elements; how exact they have to be, the bound alone decides.
A program may use at most 64 MiB of HBM per device.

```python
import jax
import jax.numpy as jnp
from jax import lax

BS = 128
K = 128
RB_DEV = 16
TILE_CAP = 24
REACH = 2
DEGREE = 4
NB = 128
NV = 16384
TILES = 192
N_BLK = 8


def draw_tile_rows(key, part):
    owner = jnp.arange(TILES, dtype=jnp.int32) // TILE_CAP
    inside = jax.random.randint(key, (TILES,), 0, RB_DEV, dtype=jnp.int32)
    return owner * RB_DEV + inside


def draw_tile_cols(key, part):
    first, second = jax.random.split(key)
    slot_index = jnp.arange(TILES, dtype=jnp.int32)
    owner = slot_index // TILE_CAP
    within = slot_index % TILE_CAP
    random_offset = jax.random.randint(first, (TILES,), -REACH, REACH + 1, dtype=jnp.int32)
    offset = jnp.where(within < 2 * REACH + 1, within - REACH, random_offset)
    inside = jax.random.randint(second, (TILES,), 0, RB_DEV, dtype=jnp.int32)
    return (owner + offset + N_BLK) % N_BLK * RB_DEV + inside


def draw_tile_counts(key, part):
    first, second, third = jax.random.split(key, 3)
    lowest = 2 * REACH + 1
    highest = max(lowest, TILE_CAP // 2)
    base = jax.random.randint(first, (N_BLK,), lowest, highest + 1, dtype=jnp.int32)
    heavy = jax.random.randint(second, (N_BLK,), 0, 8, dtype=jnp.int32) == 0
    chosen = jax.random.randint(third, (), 0, N_BLK, dtype=jnp.int32)
    heavy = heavy | (jnp.arange(N_BLK, dtype=jnp.int32) == chosen)
    return jnp.where(heavy, jnp.int32(TILE_CAP), base)


def levels(rng, dims, cuts, smallest, top_value):
    gain, own = 1.0, jax.random.fold_in(rng, 6)
    for position, shards_of in cuts:
        draws = jnp.exp(jax.random.uniform(jax.random.fold_in(own, position), (shards_of,), jnp.float32, smallest / len(cuts), top_value / len(cuts)))
        gain = gain * jnp.repeat(draws, dims[position] // shards_of).reshape([-1 if axis == position else 1 for axis in range(len(dims))])
    return gain


def bell_draw(rng, dims, width, bound, cuts=(), kind=jnp.bfloat16):
    array = jax.random.normal(rng, dims, jnp.float32) * width
    if len(cuts) > 0:
        array = levels(rng, dims, cuts, -0.22, 0.18) * array
    return jnp.clip(array, min=-bound, max=bound).astype(kind)


def setup_inputs(seed: int = 0) -> dict:
    key_list = jax.random.split(jax.random.key(seed), 6)
    return {
        "start_panel": bell_draw(key_list[0], (K, NV), 1.0, 6.0, ((0, 4), (1, 8)), jnp.float32),
        "tile_values": bell_draw(key_list[1], (TILES, BS, BS), (3 * BS) ** -0.5, 0.3125, ((0, 8),), jnp.float32),
        "tile_rows": draw_tile_rows(jax.random.fold_in(key_list[5], 71), 0),
        "tile_cols": draw_tile_cols(jax.random.fold_in(key_list[5], 71), 0),
        "tile_counts": draw_tile_counts(jax.random.fold_in(key_list[5], 71), 0),
    }


def apply_graph(panel, tile_values, tile_rows, tile_cols, tile_counts):
    blocks = panel.reshape(K, NB, BS)
    values = tile_values.reshape(N_BLK, TILE_CAP, BS, BS)
    rows = tile_rows.reshape(N_BLK, TILE_CAP)
    cols = tile_cols.reshape(N_BLK, TILE_CAP)
    slots = jnp.arange(TILE_CAP, dtype=jnp.int32)

    def step(total, item):
        vals, rws, cls, count = item
        live = slots < count
        piece = blocks[:, cls, :]
        contrib = jnp.einsum('ktb,tab->kta', piece, vals, precision=lax.Precision.HIGHEST)
        contrib = jnp.where(live[None, :, None], contrib, jnp.zeros_like(contrib))
        total = total.at[:, rws, :].add(contrib)
        return (total, None)
    start = jnp.zeros((K, NB, BS), jnp.float32).astype(panel.dtype)
    total, unused = lax.scan(step, start, (values, rows, cols, tile_counts))
    return total.reshape(K, NV)

def reference(start_panel, tile_values, tile_rows, tile_cols, tile_counts):
    previous = start_panel
    current = apply_graph(start_panel, tile_values, tile_rows, tile_cols, tile_counts)
    for step in range(DEGREE - 1):
        upcoming = 2.0 * apply_graph(current, tile_values, tile_rows, tile_cols, tile_counts) - previous
        previous, current = (current, upcoming)
    gram = jnp.dot(current, current.T, precision=lax.Precision.HIGHEST)
    factor = jnp.linalg.cholesky(gram)
    scale = jnp.sqrt(jnp.asarray(NV, jnp.float32)).astype(current.dtype)
    solved = lax.linalg.triangular_solve(factor, current, left_side=True, lower=True)
    return (solved * scale, factor / scale)
```

```python
import functools

import jax
import jax.numpy as jnp
from jax import lax
from jax.experimental import pallas as pl
from jax.experimental.pallas import tpu as pltpu
from jax.sharding import PartitionSpec as P

REACH = 2
DEGREE = 4
HALVES = 2
UNROLL = 8
MESH = pl.DeviceIdType.MESH
NT = (((1,), (1,)), ((), ()))


def split(value):
    high = value.astype(jnp.bfloat16)
    low = (value - high.astype(jnp.float32)).astype(jnp.bfloat16)
    return jnp.concatenate([high, low], axis=0)


def folded(value):
    rows, columns = value.shape[0] // 2, value.shape[1] // 2
    return (value[:rows, :columns] + value[rows:, :columns]) + (
        value[:rows, columns:] + value[rows:, columns:]
    )


def filter_kernel(
    n, q, panel_ref, tiles_ref, cols_ref, weights_ref, full_ref, gram_ref,
    weights, contrib, full, part, pair, mine, sums, rows_all,
    halo_send, halo_recv, col_send, col_recv, pair_send, pair_recv,
    sum_send, sum_recv, row_send, row_recv, *windows,
):
    win = [windows[s * HALVES:(s + 1) * HALVES] for s in range(DEGREE)]

    p, c = lax.axis_index("blk"), lax.axis_index("col")
    tiles, bs = tiles_ref.shape[0], tiles_ref.shape[1]
    width = panel_ref.shape[0]
    rb = panel_ref.shape[1] // bs
    hw = width // HALVES
    odd = lax.rem(p, 2)
    mate = p + 1 - 2 * odd
    own = REACH * rb

    def blk(value):
        return {"blk": value}

    def away(steps):
        return lax.rem(p + steps + n, n)

    core = c + 1 - 2 * lax.rem(c, 2)
    cross = lax.rem(c + 2, q)

    barrier = pltpu.get_barrier_semaphore()
    for j in range(1, n // 2):
        pl.semaphore_signal(barrier, inc=1, device_id=blk(away(2 * j)), device_id_type=MESH)
    pl.semaphore_signal(barrier, inc=1, device_id=blk(mate), device_id_type=MESH)
    for j in range(1, q):
        pl.semaphore_signal(
            barrier, inc=1, device_id={"col": lax.rem(c + j, q)}, device_id_type=MESH
        )

    for h in range(HALVES):
        for r in range(rb):
            win[0][h][own + r] = panel_ref[h * hw:(h + 1) * hw, r * bs:(r + 1) * bs]
    pl.semaphore_wait(barrier, n // 2 - 1 + 1 + q - 1)

    def slot(s, h, index):
        return win[s][h].at[pl.ds(index * rb, rb)]

    def halo(s, h, j, src, dst, target):
        return pltpu.make_async_remote_copy(
            src_ref=slot(s, h, src), dst_ref=slot(s, h, dst),
            send_sem=halo_send.at[s, h, j], recv_sem=halo_recv.at[s, h, j],
            device_id=blk(target), device_id_type=MESH,
        )

    def send(s, h):
        halo(s, h, 0, REACH, 0, away(2)).start()
        halo(s, h, 1, REACH, 4, away(-2)).start()
        halo(s, h, 2, REACH, 1 + 2 * odd, mate).start()

    def forward(s, h):
        halo(s, h, 1 - odd, REACH, 4 - 4 * odd, mate).wait_recv()
        halo(s, h, 3, 4 - 4 * odd, 3 - 2 * odd, mate).start()

    def arrived(s, h):
        halo(s, h, odd, REACH, 4 * odd, mate).wait_recv()
        halo(s, h, 2, REACH, 3 - 2 * odd, mate).wait_recv()
        halo(s, h, 3, REACH, 1 + 2 * odd, mate).wait_recv()

    def apply(s, h):
        @pl.loop(0, tiles // UNROLL)
        def _(outer):
            for u in range(UNROLL):
                t = outer * UNROLL + u
                piece = split(win[s][h][cols_ref[t]])
                contrib[t] = folded(lax.dot_general(
                    piece, weights[t], NT, preferred_element_type=jnp.float32
                ))

        @pl.loop(0, rb)
        def _(r):
            total = weights_ref[r] * contrib[0]
            for t in range(1, tiles):
                total = total + weights_ref[t * rb + r] * contrib[t]
            if s > 0:
                total = 2.0 * total - win[s - 1][h][own + r]
            if s < DEGREE - 1:
                win[s + 1][h][own + r] = total
            else:
                full[r, pl.ds(pl.multiple_of(c * width + h * hw, hw), hw), :] = total

    for h in range(HALVES):
        send(0, h)

    @pl.loop(0, tiles)
    def _(t):
        weights[t] = split(tiles_ref[t])

    def rows_of(which, h):
        return full.at[:, pl.ds(pl.multiple_of(which * width + h * hw, hw), hw), :]

    def column(h, j, which, target):
        return pltpu.make_async_remote_copy(
            src_ref=rows_of(which, h), dst_ref=rows_of(which, h),
            send_sem=col_send.at[h, j], recv_sem=col_recv.at[h, j],
            device_id={"col": target}, device_id_type=MESH,
        )

    for s in range(DEGREE):
        for h in range(HALVES):
            forward(s, h)
            arrived(s, h)
            apply(s, h)
            if s < DEGREE - 1:
                send(s + 1, h)
            else:
                column(h, 0, c, cross).start()
                column(h, 1, c, core).start()

    crossed = lax.rem(core + 2, q)
    for h in range(HALVES):
        column(h, 0, cross, cross).wait_recv()
        column(h, 2, cross, core).start()
    for h in range(HALVES):
        column(h, 1, core, core).wait_recv()
        column(h, 2, crossed, core).wait_recv()

    part[...] = jnp.zeros_like(part)

    @pl.loop(0, rb)
    def _(r):
        rows = full[r, pl.ds(pl.multiple_of(c * width, width), width), :]
        part[...] += lax.dot_general(
            split(rows), split(full[r]), NT, preferred_element_type=jnp.float32
        )

    mine[...] = folded(part[...])
    exchange = pltpu.make_async_remote_copy(
        src_ref=mine, dst_ref=pair, send_sem=pair_send, recv_sem=pair_recv,
        device_id=blk(mate), device_id_type=MESH,
    )
    exchange.start()
    exchange.wait()

    z = lax.div(p, 2)
    sums[z] = mine[...] + pair[...]

    def total_copy(j, index, target):
        return pltpu.make_async_remote_copy(
            src_ref=sums.at[index], dst_ref=sums.at[index],
            send_sem=sum_send.at[j - 1], recv_sem=sum_recv.at[j - 1],
            device_id=blk(target), device_id_type=MESH,
        )

    for j in range(1, n // 2):
        total_copy(j, z, away(2 * j)).start()
    for j in range(1, n // 2):
        total_copy(j, lax.rem(z - j + n // 2, n // 2), mate).wait_recv()
    gram = sums[0]
    for j in range(1, n // 2):
        gram = gram + sums[j]

    place = pl.ds(pl.multiple_of(c * width, width), width)
    rows_all[place, :] = gram

    def row_copy(j, which, target):
        where = rows_all.at[pl.ds(pl.multiple_of(which * width, width), width), :]
        return pltpu.make_async_remote_copy(
            src_ref=where, dst_ref=where,
            send_sem=row_send.at[j - 1], recv_sem=row_recv.at[j - 1],
            device_id={"col": target}, device_id_type=MESH,
        )

    for j in range(1, q):
        row_copy(j, c, lax.rem(c + j, q)).start()

    @pl.loop(0, rb)
    def _(r):
        full_ref[r] = full[r]

    for j in range(1, q):
        row_copy(j, lax.rem(c - j + q, q), core).wait_recv()
    gram_ref[...] = rows_all[...]

    for s in range(DEGREE):
        for h in range(HALVES):
            for j in range(4):
                halo(s, h, j, REACH, 0, mate).wait_send()
    for h in range(HALVES):
        for j in range(3):
            column(h, j, c, core).wait_send()
    for j in range(1, n // 2):
        total_copy(j, z, mate).wait_send()
    for j in range(1, q):
        row_copy(j, c, core).wait_send()


def filtered_and_gram(n, q, panel, tile_values, local_cols, row_weights):
    width, vertices = panel.shape
    tiles, bs, _ = tile_values.shape
    rb = vertices // bs
    hw = width // HALVES
    k = width * q
    dma = pltpu.SemaphoreType.DMA
    vmem = pl.BlockSpec(memory_space=pltpu.VMEM)
    smem = pl.BlockSpec(memory_space=pltpu.SMEM)
    return pl.pallas_call(
        functools.partial(filter_kernel, n, q),
        out_shape=(
            jax.ShapeDtypeStruct((rb, k, bs), jnp.float32),
            jax.ShapeDtypeStruct((k, k), jnp.float32),
        ),
        in_specs=[vmem, vmem, smem, smem],
        out_specs=(vmem, vmem),
        scratch_shapes=[
            pltpu.VMEM((tiles, 2 * bs, bs), jnp.bfloat16),
            pltpu.VMEM((tiles, hw, bs), jnp.float32),
            pltpu.VMEM((rb, k, bs), jnp.float32),
            pltpu.VMEM((2 * width, 2 * k), jnp.float32),
            pltpu.VMEM((width, k), jnp.float32),
            pltpu.VMEM((width, k), jnp.float32),
            pltpu.VMEM((n // 2, width, k), jnp.float32),
            pltpu.VMEM((k, k), jnp.float32),
            dma((DEGREE, HALVES, 4)), dma((DEGREE, HALVES, 4)),
            dma((HALVES, 3)), dma((HALVES, 3)),
            dma, dma,
            dma((n // 2 - 1,)), dma((n // 2 - 1,)),
            dma((q - 1,)), dma((q - 1,)),
        ] + [pltpu.VMEM(((2 * REACH + 1) * rb, hw, bs), jnp.float32)] * (DEGREE * HALVES),
        compiler_params=pltpu.CompilerParams(
            collective_id=0, has_side_effects=True, vmem_limit_bytes=40 << 20
        ),
    )(panel, tile_values, local_cols, row_weights)


def per_device(start_panel, tile_values, tile_rows, tile_cols, tile_counts):
    position = lax.axis_index("blk")
    n, q = lax.axis_size("blk"), lax.axis_size("col")
    width, vertices = start_panel.shape
    tiles, bs, _ = tile_values.shape
    rb = vertices // bs
    local_cols = (tile_cols // rb - position + REACH + n) % n * rb + tile_cols % rb
    local_rows = tile_rows - position * rb
    live = jnp.arange(tiles, dtype=jnp.int32) < tile_counts[0]
    row_weights = (
        (local_rows[:, None] == jnp.arange(rb, dtype=jnp.int32)[None, :]) & live[:, None]
    ).astype(jnp.float32).reshape(-1)
    full, gram = filtered_and_gram(n, q, start_panel, tile_values, local_cols, row_weights)
    factor = jnp.linalg.cholesky(gram)
    scale = jnp.sqrt(jnp.asarray(vertices * n, jnp.float32))
    inverse = lax.linalg.triangular_solve(
        factor, jnp.eye(width * q, dtype=jnp.float32), left_side=True, lower=True
    )
    inverse_rows = lax.dynamic_slice_in_dim(inverse, lax.axis_index("col") * width, width, 0)
    ortho_panel = jnp.einsum(
        "ij,bjv->ibv", inverse_rows, full, precision=lax.Precision.HIGHEST
    ).reshape(width, vertices) * scale
    return (ortho_panel, factor / scale)


def solution(mesh):
    in_specs = (P("col", "blk"), P("blk", None, None), P("blk"), P("blk"), P("blk"))
    out_specs = (P("col", "blk"), P())
    return jax.shard_map(
        per_device, mesh=mesh, in_specs=in_specs, out_specs=out_specs, check_vma=False
    )
```

```python
import functools
import math

import jax
import jax.numpy as jnp
from jax import lax
from jax.experimental import pallas as pl
from jax.experimental.pallas import tpu as pltpu
from jax.sharding import PartitionSpec as P

REACH = 2
DEGREE = 4
HALVES = 2
PIECES = 4
UNROLL = 8
MESH = pl.DeviceIdType.MESH
NT = (((1,), (1,)), ((), ()))


def split(value):
    high = value.astype(jnp.bfloat16)
    low = (value - high.astype(jnp.float32)).astype(jnp.bfloat16)
    return jnp.concatenate([high, low], axis=0)


def folded(value):
    rows, columns = value.shape[0] // 2, value.shape[1] // 2
    return (value[:rows, :columns] + value[rows:, :columns]) + (
        value[:rows, columns:] + value[rows:, columns:]
    )


def filter_kernel(
    n, q, panel_ref, tiles_ref, cols_ref, weights_ref, full_ref, gram_ref,
    weights, contrib, full, part, pair, mine, sums, rows_all,
    halo_send, halo_recv, col_send, col_recv, pair_send, pair_recv,
    sum_send, sum_recv, row_send, row_recv, *windows,
):
    win = [windows[s * HALVES:(s + 1) * HALVES] for s in range(DEGREE)]

    p, c = lax.axis_index("blk"), lax.axis_index("col")
    tiles, bs = tiles_ref.shape[0], tiles_ref.shape[1]
    width = panel_ref.shape[0]
    rb = panel_ref.shape[1] // bs
    hw = width // HALVES
    odd = lax.rem(p, 2)
    mate = p + 1 - 2 * odd
    own = REACH * rb
    span = rb // PIECES

    def blk(value):
        return {"blk": value}

    def away(steps):
        return lax.rem(p + steps + n, n)

    core = c + 1 - 2 * lax.rem(c, 2)
    cross = lax.rem(c + 2, q)

    barrier = pltpu.get_barrier_semaphore()
    for j in range(1, n // 2):
        pl.semaphore_signal(barrier, inc=1, device_id=blk(away(2 * j)), device_id_type=MESH)
    pl.semaphore_signal(barrier, inc=1, device_id=blk(mate), device_id_type=MESH)
    for j in range(1, q):
        pl.semaphore_signal(
            barrier, inc=1, device_id={"col": lax.rem(c + j, q)}, device_id_type=MESH
        )

    for h in range(HALVES):
        for r in range(rb):
            win[0][h][own + r] = panel_ref[h * hw:(h + 1) * hw, r * bs:(r + 1) * bs]
    pl.semaphore_wait(barrier, n // 2 - 1 + 1 + q - 1)

    def slot(s, h, index, piece):
        return win[s][h].at[pl.ds(index * rb + piece * span, span)]

    def halo(s, h, j, piece, src, dst, target):
        return pltpu.make_async_remote_copy(
            src_ref=slot(s, h, src, piece), dst_ref=slot(s, h, dst, piece),
            send_sem=halo_send.at[s, h, j, piece], recv_sem=halo_recv.at[s, h, j, piece],
            device_id=blk(target), device_id_type=MESH,
        )

    def send(s, h):
        for piece in range(PIECES):
            halo(s, h, 1 - odd, piece, REACH, 4 - 4 * odd, away(4 * odd - 2)).start()
            halo(s, h, odd, piece, REACH, 4 * odd, away(2 - 4 * odd)).start()
        for piece in range(PIECES):
            halo(s, h, 2, piece, REACH, 1 + 2 * odd, mate).start()

    def forward(s, h):
        for piece in range(PIECES):
            halo(s, h, 1 - odd, piece, REACH, 4 - 4 * odd, mate).wait_recv()
            halo(s, h, 3, piece, 4 - 4 * odd, 3 - 2 * odd, mate).start()

    def arrived(s, h):
        for piece in range(PIECES):
            halo(s, h, odd, piece, REACH, 4 * odd, mate).wait_recv()
            halo(s, h, 2, piece, REACH, 3 - 2 * odd, mate).wait_recv()
            halo(s, h, 3, piece, REACH, 1 + 2 * odd, mate).wait_recv()

    def apply(s, h):
        @pl.loop(0, tiles // UNROLL)
        def _(outer):
            for u in range(UNROLL):
                t = outer * UNROLL + u
                piece = split(win[s][h][cols_ref[t]])
                contrib[t] = folded(lax.dot_general(
                    piece, weights[t], NT, preferred_element_type=jnp.float32
                ))

        @pl.loop(0, rb)
        def _(r):
            total = weights_ref[r] * contrib[0]
            for t in range(1, tiles):
                total = total + weights_ref[t * rb + r] * contrib[t]
            if s > 0:
                total = 2.0 * total - win[s - 1][h][own + r]
            if s < DEGREE - 1:
                win[s + 1][h][own + r] = total
            else:
                full[r, pl.ds(pl.multiple_of(c * width + h * hw, hw), hw), :] = total

    for h in range(HALVES):
        send(0, h)

    @pl.loop(0, tiles)
    def _(t):
        weights[t] = split(tiles_ref[t])

    def rows_of(which, h):
        return full.at[:, pl.ds(pl.multiple_of(which * width + h * hw, hw), hw), :]

    def column(h, j, which, target):
        return pltpu.make_async_remote_copy(
            src_ref=rows_of(which, h), dst_ref=rows_of(which, h),
            send_sem=col_send.at[h, j], recv_sem=col_recv.at[h, j],
            device_id={"col": target}, device_id_type=MESH,
        )

    for s in range(DEGREE):
        for h in range(HALVES):
            forward(s, h)
            arrived(s, h)
            apply(s, h)
            if s < DEGREE - 1:
                send(s + 1, h)
            else:
                column(h, 0, c, cross).start()
                column(h, 1, c, core).start()

    crossed = lax.rem(core + 2, q)
    for h in range(HALVES):
        column(h, 0, cross, cross).wait_recv()
        column(h, 2, cross, core).start()
    for h in range(HALVES):
        column(h, 1, core, core).wait_recv()
        column(h, 2, crossed, core).wait_recv()

    part[...] = jnp.zeros_like(part)

    @pl.loop(0, rb)
    def _(r):
        rows = full[r, pl.ds(pl.multiple_of(c * width, width), width), :]
        part[...] += lax.dot_general(
            split(rows), split(full[r]), NT, preferred_element_type=jnp.float32
        )

    mine[...] = folded(part[...])
    exchange = pltpu.make_async_remote_copy(
        src_ref=mine, dst_ref=pair, send_sem=pair_send, recv_sem=pair_recv,
        device_id=blk(mate), device_id_type=MESH,
    )
    exchange.start()
    exchange.wait()

    z = lax.div(p, 2)
    sums[z] = mine[...] + pair[...]

    def total_copy(j, index, target):
        return pltpu.make_async_remote_copy(
            src_ref=sums.at[index], dst_ref=sums.at[index],
            send_sem=sum_send.at[j - 1], recv_sem=sum_recv.at[j - 1],
            device_id=blk(target), device_id_type=MESH,
        )

    for j in range(1, n // 2):
        total_copy(j, z, away(2 * j)).start()
    for j in range(1, n // 2):
        total_copy(j, lax.rem(z - j + n // 2, n // 2), mate).wait_recv()
    gram = sums[0]
    for j in range(1, n // 2):
        gram = gram + sums[j]

    place = pl.ds(pl.multiple_of(c * width, width), width)
    rows_all[place, :] = gram

    def row_copy(j, which, target):
        where = rows_all.at[pl.ds(pl.multiple_of(which * width, width), width), :]
        return pltpu.make_async_remote_copy(
            src_ref=where, dst_ref=where,
            send_sem=row_send.at[j - 1], recv_sem=row_recv.at[j - 1],
            device_id={"col": target}, device_id_type=MESH,
        )

    for j in range(1, q):
        row_copy(j, c, lax.rem(c + j, q)).start()

    @pl.loop(0, rb)
    def _(r):
        full_ref[r] = full[r]

    for j in range(1, q):
        row_copy(j, lax.rem(c - j + q, q), core).wait_recv()
    gram_ref[...] = rows_all[...]

    for s in range(DEGREE):
        for h in range(HALVES):
            for j in range(4):
                for piece in range(PIECES):
                    halo(s, h, j, piece, REACH, 0, mate).wait_send()
    for h in range(HALVES):
        for j in range(3):
            column(h, j, c, core).wait_send()
    for j in range(1, n // 2):
        total_copy(j, z, mate).wait_send()
    for j in range(1, q):
        row_copy(j, c, core).wait_send()


def filtered_and_gram(n, q, panel, tile_values, local_cols, row_weights):
    width, vertices = panel.shape
    tiles, bs, _ = tile_values.shape
    rb = vertices // bs
    hw = width // HALVES
    k = width * q
    dma = pltpu.SemaphoreType.DMA
    vmem = pl.BlockSpec(memory_space=pltpu.VMEM)
    smem = pl.BlockSpec(memory_space=pltpu.SMEM)
    return pl.pallas_call(
        functools.partial(filter_kernel, n, q),
        out_shape=(
            jax.ShapeDtypeStruct((rb, k, bs), jnp.float32),
            jax.ShapeDtypeStruct((k, k), jnp.float32),
        ),
        in_specs=[vmem, vmem, smem, smem],
        out_specs=(vmem, vmem),
        scratch_shapes=[
            pltpu.VMEM((tiles, 2 * bs, bs), jnp.bfloat16),
            pltpu.VMEM((tiles, hw, bs), jnp.float32),
            pltpu.VMEM((rb, k, bs), jnp.float32),
            pltpu.VMEM((2 * width, 2 * k), jnp.float32),
            pltpu.VMEM((width, k), jnp.float32),
            pltpu.VMEM((width, k), jnp.float32),
            pltpu.VMEM((n // 2, width, k), jnp.float32),
            pltpu.VMEM((k, k), jnp.float32),
            dma((DEGREE, HALVES, 4, PIECES)), dma((DEGREE, HALVES, 4, PIECES)),
            dma((HALVES, 3)), dma((HALVES, 3)),
            dma, dma,
            dma((n // 2 - 1,)), dma((n // 2 - 1,)),
            dma((q - 1,)), dma((q - 1,)),
        ] + [pltpu.VMEM(((2 * REACH + 1) * rb, hw, bs), jnp.float32)] * (DEGREE * HALVES),
        compiler_params=pltpu.CompilerParams(
            collective_id=0, has_side_effects=True, vmem_limit_bytes=40 << 20
        ),
    )(panel, tile_values, local_cols, row_weights)


def split_three(value):
    first = value.astype(jnp.bfloat16)
    rest = value - first.astype(jnp.float32)
    second = rest.astype(jnp.bfloat16)
    third = (rest - second.astype(jnp.float32)).astype(jnp.bfloat16)
    return first, second, third


def factor_kernel(root, gram_ref, full_ref, ortho_ref, factor_ref, work, upper, inverse):
    k = gram_ref.shape[0]
    rb, bs = full_ref.shape[0], full_ref.shape[2]
    width = ortho_ref.shape[0]
    group = 8
    row_index = lax.broadcasted_iota(jnp.int32, (k, k), 0)
    lane_index = lax.broadcasted_iota(jnp.int32, (k, k), 1)
    work[:, :k] = gram_ref[...]
    work[:, k:] = jnp.where(row_index == lane_index, 1.0, 0.0)
    sub = lax.broadcasted_iota(jnp.int32, (group, k), 0)
    lane = lax.broadcasted_iota(jnp.int32, (group, k), 1)
    for start in range(0, k, group):
        left = work[start:start + group, :k]
        right = work[start:start + group, k:]
        columns = [
            jnp.broadcast_to(left[:, start + j:start + j + 1], (group, k)) for j in range(group)
        ]
        pivots = jnp.ones((group, k), jnp.float32)
        for j in range(group):
            pivot = jnp.broadcast_to(columns[j][j:j + 1, :], (group, k))
            pivots = jnp.where(sub == j, pivot, pivots)
            if j < group - 1:
                factor = jnp.where(sub > j, columns[j] / pivot, 0.0)
                for m in range(j + 1, group):
                    columns[m] = columns[m] - factor * columns[m][j:j + 1, :]
                left = left - factor * left[j:j + 1, :]
                right = right - factor * right[j:j + 1, :]
        scale = lax.rsqrt(pivots)
        scale = scale * (1.5 - (0.5 * pivots * scale) * scale)
        left = jnp.where(lane >= sub + start, left * scale, 0.0)
        right = right * scale
        upper[start:start + group, :] = left
        inverse[start:start + group, :] = right
        if start + group < k:
            a, b, c = split_three(left)
            x, y, z = split_three(jnp.concatenate([left, right], axis=1))
            work[...] -= lax.dot_general(
                jnp.concatenate([a, a, b, a, b, c], axis=0),
                jnp.concatenate([x, y, x, z, y, x], axis=0),
                (((0,), (0,)), ((), ())), preferred_element_type=jnp.float32,
            )
    factor_ref[...] = upper[...].T * (1.0 / root)
    place = pl.ds(pl.multiple_of(lax.axis_index("col") * width, width), width)
    rows = split(inverse[place, :] * root)
    for r in range(rb):
        block = full_ref[r]
        high = block.astype(jnp.bfloat16)
        low = (block - high.astype(jnp.float32)).astype(jnp.bfloat16)
        ortho_ref[:, r * bs:(r + 1) * bs] = folded(jnp.dot(
            rows, jnp.concatenate([high, low], axis=1), preferred_element_type=jnp.float32
        ))


def factor_and_ortho(root, width, gram, full):
    k = gram.shape[0]
    rb, _, bs = full.shape
    vmem = pl.BlockSpec(memory_space=pltpu.VMEM)
    return pl.pallas_call(
        functools.partial(factor_kernel, root),
        out_shape=(
            jax.ShapeDtypeStruct((width, rb * bs), jnp.float32),
            jax.ShapeDtypeStruct((k, k), jnp.float32),
        ),
        in_specs=[vmem, vmem],
        out_specs=(vmem, vmem),
        scratch_shapes=[
            pltpu.VMEM((k, 2 * k), jnp.float32),
            pltpu.VMEM((k, k), jnp.float32),
            pltpu.VMEM((k, k), jnp.float32),
        ],
        compiler_params=pltpu.CompilerParams(vmem_limit_bytes=24 << 20),
    )(gram, full)


def per_device(start_panel, tile_values, tile_rows, tile_cols, tile_counts):
    position = lax.axis_index("blk")
    n, q = lax.axis_size("blk"), lax.axis_size("col")
    width, vertices = start_panel.shape
    tiles, bs, _ = tile_values.shape
    rb = vertices // bs
    local_cols = (tile_cols // rb - position + REACH + n) % n * rb + tile_cols % rb
    local_rows = tile_rows - position * rb
    live = jnp.arange(tiles, dtype=jnp.int32) < tile_counts[0]
    row_weights = (
        (local_rows[:, None] == jnp.arange(rb, dtype=jnp.int32)[None, :]) & live[:, None]
    ).astype(jnp.float32).reshape(-1)
    full, gram = filtered_and_gram(n, q, start_panel, tile_values, local_cols, row_weights)
    return factor_and_ortho(math.sqrt(vertices * n), width, gram, full)


def solution(mesh):
    in_specs = (P("col", "blk"), P("blk", None, None), P("blk"), P("blk"), P("blk"))
    out_specs = (P("col", "blk"), P())
    return jax.shard_map(
        per_device, mesh=mesh, in_specs=in_specs, out_specs=out_specs, check_vma=False
    )
```

```python
import functools
import math

import jax
import jax.numpy as jnp
from jax import lax
from jax.experimental import pallas as pl
from jax.experimental.pallas import tpu as pltpu
from jax.sharding import PartitionSpec as P

REACH = 2
DEGREE = 4
HALVES = 2
PIECES = 4
UNROLL = 8
MESH = pl.DeviceIdType.MESH
NT = (((1,), (1,)), ((), ()))


def split(value):
    high = value.astype(jnp.bfloat16)
    low = (value - high.astype(jnp.float32)).astype(jnp.bfloat16)
    return jnp.concatenate([high, low], axis=0)


def folded(value):
    rows, columns = value.shape[0] // 2, value.shape[1] // 2
    return (value[:rows, :columns] + value[rows:, :columns]) + (
        value[:rows, columns:] + value[rows:, columns:]
    )


def filter_kernel(
    n, q, panel_ref, tiles_ref, cols_ref, weights_ref, full_ref, gram_ref,
    weights, contrib, full, part, pair, mine, sums, rows_all,
    halo_send, halo_recv, col_send, col_recv, pair_send, pair_recv,
    sum_send, sum_recv, row_send, row_recv, *windows,
):
    win = [windows[s * HALVES:(s + 1) * HALVES] for s in range(DEGREE)]

    p, c = lax.axis_index("blk"), lax.axis_index("col")
    tiles, bs = tiles_ref.shape[0], tiles_ref.shape[1]
    width = panel_ref.shape[0]
    rb = panel_ref.shape[1] // bs
    hw = width // HALVES
    odd = lax.rem(p, 2)
    mate = p + 1 - 2 * odd
    own = REACH * rb
    span = rb // PIECES

    def blk(value):
        return {"blk": value}

    def away(steps):
        return lax.rem(p + steps + n, n)

    core = c + 1 - 2 * lax.rem(c, 2)
    cross = lax.rem(c + 2, q)

    barrier = pltpu.get_barrier_semaphore()
    for j in range(1, n // 2):
        pl.semaphore_signal(barrier, inc=1, device_id=blk(away(2 * j)), device_id_type=MESH)
    pl.semaphore_signal(barrier, inc=1, device_id=blk(mate), device_id_type=MESH)
    for j in range(1, q):
        pl.semaphore_signal(
            barrier, inc=1, device_id={"col": lax.rem(c + j, q)}, device_id_type=MESH
        )

    for h in range(HALVES):
        for r in range(rb):
            win[0][h][own + r] = panel_ref[h * hw:(h + 1) * hw, r * bs:(r + 1) * bs]
    pl.semaphore_wait(barrier, n // 2 - 1 + 1 + q - 1)

    def slot(s, h, index, piece):
        return win[s][h].at[pl.ds(index * rb + piece * span, span)]

    def halo(s, h, j, piece, src, dst, target):
        return pltpu.make_async_remote_copy(
            src_ref=slot(s, h, src, piece), dst_ref=slot(s, h, dst, piece),
            send_sem=halo_send.at[s, h, j, piece], recv_sem=halo_recv.at[s, h, j, piece],
            device_id=blk(target), device_id_type=MESH,
        )

    def send(s, h):
        for piece in range(PIECES):
            halo(s, h, 1 - odd, piece, REACH, 4 - 4 * odd, away(4 * odd - 2)).start()
            halo(s, h, odd, piece, REACH, 4 * odd, away(2 - 4 * odd)).start()

    def send_mate(s, h):
        for piece in range(PIECES):
            halo(s, h, 2, piece, REACH, 1 + 2 * odd, mate).start()

    def forward(s, h):
        for piece in range(PIECES):
            halo(s, h, 1 - odd, piece, REACH, 4 - 4 * odd, mate).wait_recv()
            halo(s, h, 3, piece, 4 - 4 * odd, 3 - 2 * odd, mate).start()

    def arrived(s, h):
        for piece in range(PIECES):
            halo(s, h, odd, piece, REACH, 4 * odd, mate).wait_recv()
            halo(s, h, 2, piece, REACH, 3 - 2 * odd, mate).wait_recv()
            halo(s, h, 3, piece, REACH, 1 + 2 * odd, mate).wait_recv()

    def apply(s, h):
        @pl.loop(0, tiles // UNROLL)
        def _(outer):
            for u in range(UNROLL):
                t = outer * UNROLL + u
                piece = split(win[s][h][cols_ref[t]])
                contrib[t] = folded(lax.dot_general(
                    piece, weights[t], NT, preferred_element_type=jnp.float32
                ))

        @pl.loop(0, rb)
        def _(r):
            total = weights_ref[r] * contrib[0]
            for t in range(1, tiles):
                total = total + weights_ref[t * rb + r] * contrib[t]
            if s > 0:
                total = 2.0 * total - win[s - 1][h][own + r]
            if s < DEGREE - 1:
                win[s + 1][h][own + r] = total
            else:
                full[r, pl.ds(pl.multiple_of(c * width + h * hw, hw), hw), :] = total

    for h in range(HALVES):
        send(0, h)
        send_mate(0, h)

    @pl.loop(0, tiles)
    def _(t):
        weights[t] = split(tiles_ref[t])

    def rows_of(which, h):
        return full.at[:, pl.ds(pl.multiple_of(which * width + h * hw, hw), hw), :]

    def column(h, j, which, target):
        return pltpu.make_async_remote_copy(
            src_ref=rows_of(which, h), dst_ref=rows_of(which, h),
            send_sem=col_send.at[h, j], recv_sem=col_recv.at[h, j],
            device_id={"col": target}, device_id_type=MESH,
        )

    forward(0, 0)
    for s in range(DEGREE):
        for h in range(HALVES):
            arrived(s, h)
            apply(s, h)
            if s < DEGREE - 1:
                send(s + 1, h)
            else:
                column(h, 0, c, cross).start()
                column(h, 1, c, core).start()
            if h < HALVES - 1:
                forward(s, h + 1)
            elif s < DEGREE - 1:
                forward(s + 1, 0)
            if s < DEGREE - 1:
                send_mate(s + 1, h)

    crossed = lax.rem(core + 2, q)
    for h in range(HALVES):
        column(h, 0, cross, cross).wait_recv()
        column(h, 2, cross, core).start()
    for h in range(HALVES):
        column(h, 1, core, core).wait_recv()
        column(h, 2, crossed, core).wait_recv()

    part[...] = jnp.zeros_like(part)

    @pl.loop(0, rb)
    def _(r):
        rows = full[r, pl.ds(pl.multiple_of(c * width, width), width), :]
        part[...] += lax.dot_general(
            split(rows), split(full[r]), NT, preferred_element_type=jnp.float32
        )

    mine[...] = folded(part[...])
    exchange = pltpu.make_async_remote_copy(
        src_ref=mine, dst_ref=pair, send_sem=pair_send, recv_sem=pair_recv,
        device_id=blk(mate), device_id_type=MESH,
    )
    exchange.start()
    exchange.wait()

    z = lax.div(p, 2)
    sums[z] = mine[...] + pair[...]

    def total_copy(j, index, target):
        return pltpu.make_async_remote_copy(
            src_ref=sums.at[index], dst_ref=sums.at[index],
            send_sem=sum_send.at[j - 1], recv_sem=sum_recv.at[j - 1],
            device_id=blk(target), device_id_type=MESH,
        )

    for j in range(1, n // 2):
        total_copy(j, z, away(2 * j)).start()
    for j in range(1, n // 2):
        total_copy(j, lax.rem(z - j + n // 2, n // 2), mate).wait_recv()
    gram = sums[0]
    for j in range(1, n // 2):
        gram = gram + sums[j]

    place = pl.ds(pl.multiple_of(c * width, width), width)
    rows_all[place, :] = gram

    def row_copy(j, which, target):
        where = rows_all.at[pl.ds(pl.multiple_of(which * width, width), width), :]
        return pltpu.make_async_remote_copy(
            src_ref=where, dst_ref=where,
            send_sem=row_send.at[j - 1], recv_sem=row_recv.at[j - 1],
            device_id={"col": target}, device_id_type=MESH,
        )

    for j in range(1, q):
        row_copy(j, c, lax.rem(c + j, q)).start()

    @pl.loop(0, rb)
    def _(r):
        full_ref[r] = full[r]

    for j in range(1, q):
        row_copy(j, lax.rem(c - j + q, q), core).wait_recv()
    gram_ref[...] = rows_all[...]

    for s in range(DEGREE):
        for h in range(HALVES):
            for j in range(4):
                for piece in range(PIECES):
                    halo(s, h, j, piece, REACH, 0, mate).wait_send()
    for h in range(HALVES):
        for j in range(3):
            column(h, j, c, core).wait_send()
    for j in range(1, n // 2):
        total_copy(j, z, mate).wait_send()
    for j in range(1, q):
        row_copy(j, c, core).wait_send()


def filtered_and_gram(n, q, panel, tile_values, local_cols, row_weights):
    width, vertices = panel.shape
    tiles, bs, _ = tile_values.shape
    rb = vertices // bs
    hw = width // HALVES
    k = width * q
    dma = pltpu.SemaphoreType.DMA
    vmem = pl.BlockSpec(memory_space=pltpu.VMEM)
    smem = pl.BlockSpec(memory_space=pltpu.SMEM)
    return pl.pallas_call(
        functools.partial(filter_kernel, n, q),
        out_shape=(
            jax.ShapeDtypeStruct((rb, k, bs), jnp.float32),
            jax.ShapeDtypeStruct((k, k), jnp.float32),
        ),
        in_specs=[vmem, vmem, smem, smem],
        out_specs=(vmem, vmem),
        scratch_shapes=[
            pltpu.VMEM((tiles, 2 * bs, bs), jnp.bfloat16),
            pltpu.VMEM((tiles, hw, bs), jnp.float32),
            pltpu.VMEM((rb, k, bs), jnp.float32),
            pltpu.VMEM((2 * width, 2 * k), jnp.float32),
            pltpu.VMEM((width, k), jnp.float32),
            pltpu.VMEM((width, k), jnp.float32),
            pltpu.VMEM((n // 2, width, k), jnp.float32),
            pltpu.VMEM((k, k), jnp.float32),
            dma((DEGREE, HALVES, 4, PIECES)), dma((DEGREE, HALVES, 4, PIECES)),
            dma((HALVES, 3)), dma((HALVES, 3)),
            dma, dma,
            dma((n // 2 - 1,)), dma((n // 2 - 1,)),
            dma((q - 1,)), dma((q - 1,)),
        ] + [pltpu.VMEM(((2 * REACH + 1) * rb, hw, bs), jnp.float32)] * (DEGREE * HALVES),
        compiler_params=pltpu.CompilerParams(
            collective_id=0, has_side_effects=True, vmem_limit_bytes=40 << 20
        ),
    )(panel, tile_values, local_cols, row_weights)


def split_three(value):
    first = value.astype(jnp.bfloat16)
    rest = value - first.astype(jnp.float32)
    second = rest.astype(jnp.bfloat16)
    third = (rest - second.astype(jnp.float32)).astype(jnp.bfloat16)
    return first, second, third


def factor_kernel(root, gram_ref, full_ref, ortho_ref, factor_ref, work, upper, inverse):
    k = gram_ref.shape[0]
    rb, bs = full_ref.shape[0], full_ref.shape[2]
    width = ortho_ref.shape[0]
    group = 8
    row_index = lax.broadcasted_iota(jnp.int32, (k, k), 0)
    lane_index = lax.broadcasted_iota(jnp.int32, (k, k), 1)
    work[:, :k] = gram_ref[...]
    work[:, k:] = jnp.where(row_index == lane_index, 1.0, 0.0)
    sub = lax.broadcasted_iota(jnp.int32, (group, k), 0)
    lane = lax.broadcasted_iota(jnp.int32, (group, k), 1)
    for start in range(0, k, group):
        left = work[start:start + group, :k]
        right = work[start:start + group, k:]
        columns = [
            jnp.broadcast_to(left[:, start + j:start + j + 1], (group, k)) for j in range(group)
        ]
        pivots = jnp.ones((group, k), jnp.float32)
        for j in range(group):
            pivot = jnp.broadcast_to(columns[j][j:j + 1, :], (group, k))
            pivots = jnp.where(sub == j, pivot, pivots)
            if j < group - 1:
                factor = jnp.where(sub > j, columns[j] / pivot, 0.0)
                for m in range(j + 1, group):
                    columns[m] = columns[m] - factor * columns[m][j:j + 1, :]
                left = left - factor * left[j:j + 1, :]
                right = right - factor * right[j:j + 1, :]
        scale = lax.rsqrt(pivots)
        scale = scale * (1.5 - (0.5 * pivots * scale) * scale)
        left = jnp.where(lane >= sub + start, left * scale, 0.0)
        right = right * scale
        upper[start:start + group, :] = left
        inverse[start:start + group, :] = right
        if start + group < k:
            a, b, c = split_three(left)
            x, y, z = split_three(jnp.concatenate([left, right], axis=1))
            work[...] -= lax.dot_general(
                jnp.concatenate([a, a, b, a, b, c], axis=0),
                jnp.concatenate([x, y, x, z, y, x], axis=0),
                (((0,), (0,)), ((), ())), preferred_element_type=jnp.float32,
            )
    factor_ref[...] = upper[...].T * (1.0 / root)
    place = pl.ds(pl.multiple_of(lax.axis_index("col") * width, width), width)
    rows = split(inverse[place, :] * root)
    for r in range(rb):
        block = full_ref[r]
        high = block.astype(jnp.bfloat16)
        low = (block - high.astype(jnp.float32)).astype(jnp.bfloat16)
        ortho_ref[:, r * bs:(r + 1) * bs] = folded(jnp.dot(
            rows, jnp.concatenate([high, low], axis=1), preferred_element_type=jnp.float32
        ))


def factor_and_ortho(root, width, gram, full):
    k = gram.shape[0]
    rb, _, bs = full.shape
    vmem = pl.BlockSpec(memory_space=pltpu.VMEM)
    return pl.pallas_call(
        functools.partial(factor_kernel, root),
        out_shape=(
            jax.ShapeDtypeStruct((width, rb * bs), jnp.float32),
            jax.ShapeDtypeStruct((k, k), jnp.float32),
        ),
        in_specs=[vmem, vmem],
        out_specs=(vmem, vmem),
        scratch_shapes=[
            pltpu.VMEM((k, 2 * k), jnp.float32),
            pltpu.VMEM((k, k), jnp.float32),
            pltpu.VMEM((k, k), jnp.float32),
        ],
        compiler_params=pltpu.CompilerParams(vmem_limit_bytes=24 << 20),
    )(gram, full)


def per_device(start_panel, tile_values, tile_rows, tile_cols, tile_counts):
    position = lax.axis_index("blk")
    n, q = lax.axis_size("blk"), lax.axis_size("col")
    width, vertices = start_panel.shape
    tiles, bs, _ = tile_values.shape
    rb = vertices // bs
    local_cols = (tile_cols // rb - position + REACH + n) % n * rb + tile_cols % rb
    local_rows = tile_rows - position * rb
    live = jnp.arange(tiles, dtype=jnp.int32) < tile_counts[0]
    row_weights = (
        (local_rows[:, None] == jnp.arange(rb, dtype=jnp.int32)[None, :]) & live[:, None]
    ).astype(jnp.float32).reshape(-1)
    full, gram = filtered_and_gram(n, q, start_panel, tile_values, local_cols, row_weights)
    return factor_and_ortho(math.sqrt(vertices * n), width, gram, full)


def solution(mesh):
    in_specs = (P("col", "blk"), P("blk", None, None), P("blk"), P("blk"), P("blk"))
    out_specs = (P("col", "blk"), P())
    return jax.shard_map(
        per_device, mesh=mesh, in_specs=in_specs, out_specs=out_specs, check_vma=False
    )
```

```python
import functools
import math

import jax
import jax.numpy as jnp
from jax import lax
from jax.experimental import pallas as pl
from jax.experimental.pallas import tpu as pltpu
from jax.sharding import PartitionSpec as P

REACH = 2
DEGREE = 4
HALVES = 2
PIECES = 2
UNROLL = 8
MESH = pl.DeviceIdType.MESH
NT = (((1,), (1,)), ((), ()))


def split(value):
    high = value.astype(jnp.bfloat16)
    low = (value - high.astype(jnp.float32)).astype(jnp.bfloat16)
    return jnp.concatenate([high, low], axis=0)


def folded(value):
    rows, columns = value.shape[0] // 2, value.shape[1] // 2
    return (value[:rows, :columns] + value[rows:, :columns]) + (
        value[:rows, columns:] + value[rows:, columns:]
    )


def filter_kernel(
    n, q, panel_ref, tiles_hbm, cols_ref, weights_ref, full_ref, gram_ref,
    tiles_ref, tiles_sem, weights, contrib, full, part, pair, mine, sums, rows_all,
    halo_send, halo_recv, col_send, col_recv, pair_send, pair_recv,
    sum_send, sum_recv, row_send, row_recv, *windows,
):
    win = [windows[s * HALVES:(s + 1) * HALVES] for s in range(DEGREE)]

    p, c = lax.axis_index("blk"), lax.axis_index("col")
    tiles, bs = tiles_ref.shape[0], tiles_ref.shape[1]
    width = panel_ref.shape[0]
    rb = panel_ref.shape[1] // bs
    hw = width // HALVES
    odd = lax.rem(p, 2)
    mate = p + 1 - 2 * odd
    own = REACH * rb
    span = rb // PIECES

    def blk(value):
        return {"blk": value}

    def away(steps):
        return lax.rem(p + steps + n, n)

    core = c + 1 - 2 * lax.rem(c, 2)
    cross = lax.rem(c + 2, q)

    fetch = pltpu.make_async_copy(tiles_hbm, tiles_ref, tiles_sem)
    fetch.start()
    barrier = pltpu.get_barrier_semaphore()
    for j in range(1, n // 2):
        pl.semaphore_signal(barrier, inc=1, device_id=blk(away(2 * j)), device_id_type=MESH)
    pl.semaphore_signal(barrier, inc=1, device_id=blk(mate), device_id_type=MESH)
    for j in range(1, q):
        pl.semaphore_signal(
            barrier, inc=1, device_id={"col": lax.rem(c + j, q)}, device_id_type=MESH
        )

    for h in range(HALVES):
        for r in range(rb):
            win[0][h][own + r] = panel_ref[h * hw:(h + 1) * hw, r * bs:(r + 1) * bs]
    pl.semaphore_wait(barrier, n // 2 - 1 + 1 + q - 1)

    def slot(s, h, index, piece):
        return win[s][h].at[pl.ds(index * rb + piece * span, span)]

    def halo(s, h, j, piece, src, dst, target):
        return pltpu.make_async_remote_copy(
            src_ref=slot(s, h, src, piece), dst_ref=slot(s, h, dst, piece),
            send_sem=halo_send.at[s, h, j, piece], recv_sem=halo_recv.at[s, h, j, piece],
            device_id=blk(target), device_id_type=MESH,
        )

    def send(s, h):
        for piece in range(PIECES):
            halo(s, h, 1 - odd, piece, REACH, 4 - 4 * odd, away(4 * odd - 2)).start()
            halo(s, h, odd, piece, REACH, 4 * odd, away(2 - 4 * odd)).start()

    def send_mate(s, h):
        for piece in range(PIECES):
            halo(s, h, 2, piece, REACH, 1 + 2 * odd, mate).start()

    def forward(s, h):
        for piece in range(PIECES):
            halo(s, h, 1 - odd, piece, REACH, 4 - 4 * odd, mate).wait_recv()
            halo(s, h, 3, piece, 4 - 4 * odd, 3 - 2 * odd, mate).start()

    def arrived(s, h):
        for piece in range(PIECES):
            halo(s, h, odd, piece, REACH, 4 * odd, mate).wait_recv()
            halo(s, h, 2, piece, REACH, 3 - 2 * odd, mate).wait_recv()
            halo(s, h, 3, piece, REACH, 1 + 2 * odd, mate).wait_recv()

    def apply(s, h):
        @pl.loop(0, tiles // UNROLL)
        def _(outer):
            for u in range(UNROLL):
                t = outer * UNROLL + u
                piece = split(win[s][h][cols_ref[t]])
                contrib[t] = folded(lax.dot_general(
                    piece, weights[t], NT, preferred_element_type=jnp.float32
                ))

        @pl.loop(0, rb)
        def _(r):
            total = weights_ref[r] * contrib[0]
            for t in range(1, tiles):
                total = total + weights_ref[t * rb + r] * contrib[t]
            if s > 0:
                total = 2.0 * total - win[s - 1][h][own + r]
            if s < DEGREE - 1:
                win[s + 1][h][own + r] = total
            else:
                full[r, pl.ds(pl.multiple_of(c * width + h * hw, hw), hw), :] = total

    for h in range(HALVES):
        send(0, h)
        send_mate(0, h)

    fetch.wait()

    @pl.loop(0, tiles)
    def _(t):
        weights[t] = split(tiles_ref[t])

    def rows_of(which, h):
        return full.at[:, pl.ds(pl.multiple_of(which * width + h * hw, hw), hw), :]

    def column(h, j, which, target):
        return pltpu.make_async_remote_copy(
            src_ref=rows_of(which, h), dst_ref=rows_of(which, h),
            send_sem=col_send.at[h, j], recv_sem=col_recv.at[h, j],
            device_id={"col": target}, device_id_type=MESH,
        )

    forward(0, 0)
    for s in range(DEGREE):
        for h in range(HALVES):
            arrived(s, h)
            apply(s, h)
            if s < DEGREE - 1:
                send(s + 1, h)
            else:
                column(h, 0, c, cross).start()
                column(h, 1, c, core).start()
            if h < HALVES - 1:
                forward(s, h + 1)
            elif s < DEGREE - 1:
                forward(s + 1, 0)
            if s < DEGREE - 1:
                send_mate(s + 1, h)

    crossed = lax.rem(core + 2, q)
    for h in range(HALVES):
        column(h, 0, cross, cross).wait_recv()
        column(h, 2, cross, core).start()
    for h in range(HALVES):
        column(h, 1, core, core).wait_recv()
        column(h, 2, crossed, core).wait_recv()

    part[...] = jnp.zeros_like(part)

    @pl.loop(0, rb)
    def _(r):
        rows = full[r, pl.ds(pl.multiple_of(c * width, width), width), :]
        part[...] += lax.dot_general(
            split(rows), split(full[r]), NT, preferred_element_type=jnp.float32
        )

    mine[...] = folded(part[...])
    exchange = pltpu.make_async_remote_copy(
        src_ref=mine, dst_ref=pair, send_sem=pair_send, recv_sem=pair_recv,
        device_id=blk(mate), device_id_type=MESH,
    )
    exchange.start()
    exchange.wait()

    z = lax.div(p, 2)
    sums[z] = mine[...] + pair[...]

    def total_copy(j, index, target):
        return pltpu.make_async_remote_copy(
            src_ref=sums.at[index], dst_ref=sums.at[index],
            send_sem=sum_send.at[j - 1], recv_sem=sum_recv.at[j - 1],
            device_id=blk(target), device_id_type=MESH,
        )

    for j in range(1, n // 2):
        total_copy(j, z, away(2 * j)).start()
    for j in range(1, n // 2):
        total_copy(j, lax.rem(z - j + n // 2, n // 2), mate).wait_recv()
    gram = sums[0]
    for j in range(1, n // 2):
        gram = gram + sums[j]

    place = pl.ds(pl.multiple_of(c * width, width), width)
    rows_all[place, :] = gram

    def row_copy(j, which, target):
        where = rows_all.at[pl.ds(pl.multiple_of(which * width, width), width), :]
        return pltpu.make_async_remote_copy(
            src_ref=where, dst_ref=where,
            send_sem=row_send.at[j - 1], recv_sem=row_recv.at[j - 1],
            device_id={"col": target}, device_id_type=MESH,
        )

    for j in range(1, q):
        row_copy(j, c, lax.rem(c + j, q)).start()

    @pl.loop(0, rb)
    def _(r):
        full_ref[r] = full[r]

    for j in range(1, q):
        row_copy(j, lax.rem(c - j + q, q), core).wait_recv()
    gram_ref[...] = rows_all[...]

    for s in range(DEGREE):
        for h in range(HALVES):
            for j in range(4):
                for piece in range(PIECES):
                    halo(s, h, j, piece, REACH, 0, mate).wait_send()
    for h in range(HALVES):
        for j in range(3):
            column(h, j, c, core).wait_send()
    for j in range(1, n // 2):
        total_copy(j, z, mate).wait_send()
    for j in range(1, q):
        row_copy(j, c, core).wait_send()


def filtered_and_gram(n, q, panel, tile_values, local_cols, row_weights):
    width, vertices = panel.shape
    tiles, bs, _ = tile_values.shape
    rb = vertices // bs
    hw = width // HALVES
    k = width * q
    dma = pltpu.SemaphoreType.DMA
    vmem = pl.BlockSpec(memory_space=pltpu.VMEM)
    smem = pl.BlockSpec(memory_space=pltpu.SMEM)
    return pl.pallas_call(
        functools.partial(filter_kernel, n, q),
        out_shape=(
            jax.ShapeDtypeStruct((rb, k, bs), jnp.float32),
            jax.ShapeDtypeStruct((k, k), jnp.float32),
        ),
        in_specs=[vmem, pl.BlockSpec(memory_space=pltpu.HBM), smem, smem],
        out_specs=(vmem, vmem),
        scratch_shapes=[
            pltpu.VMEM((tiles, bs, bs), jnp.float32), dma,
            pltpu.VMEM((tiles, 2 * bs, bs), jnp.bfloat16),
            pltpu.VMEM((tiles, hw, bs), jnp.float32),
            pltpu.VMEM((rb, k, bs), jnp.float32),
            pltpu.VMEM((2 * width, 2 * k), jnp.float32),
            pltpu.VMEM((width, k), jnp.float32),
            pltpu.VMEM((width, k), jnp.float32),
            pltpu.VMEM((n // 2, width, k), jnp.float32),
            pltpu.VMEM((k, k), jnp.float32),
            dma((DEGREE, HALVES, 4, PIECES)), dma((DEGREE, HALVES, 4, PIECES)),
            dma((HALVES, 3)), dma((HALVES, 3)),
            dma, dma,
            dma((n // 2 - 1,)), dma((n // 2 - 1,)),
            dma((q - 1,)), dma((q - 1,)),
        ] + [pltpu.VMEM(((2 * REACH + 1) * rb, hw, bs), jnp.float32)] * (DEGREE * HALVES),
        compiler_params=pltpu.CompilerParams(
            collective_id=0, has_side_effects=True, vmem_limit_bytes=40 << 20
        ),
    )(panel, tile_values, local_cols, row_weights)


def split_three(value):
    first = value.astype(jnp.bfloat16)
    rest = value - first.astype(jnp.float32)
    second = rest.astype(jnp.bfloat16)
    third = (rest - second.astype(jnp.float32)).astype(jnp.bfloat16)
    return first, second, third


def factor_kernel(root, gram_ref, full_ref, ortho_ref, factor_ref, work, upper, inverse):
    k = gram_ref.shape[0]
    rb, bs = full_ref.shape[0], full_ref.shape[2]
    width = ortho_ref.shape[0]
    group = 8
    row_index = lax.broadcasted_iota(jnp.int32, (k, k), 0)
    lane_index = lax.broadcasted_iota(jnp.int32, (k, k), 1)
    work[:, :k] = gram_ref[...]
    work[:, k:] = jnp.where(row_index == lane_index, 1.0, 0.0)
    sub = lax.broadcasted_iota(jnp.int32, (group, k), 0)
    lane = lax.broadcasted_iota(jnp.int32, (group, k), 1)
    for start in range(0, k, group):
        left = work[start:start + group, :k]
        right = work[start:start + group, k:]
        columns = [
            jnp.broadcast_to(left[:, start + j:start + j + 1], (group, k)) for j in range(group)
        ]
        pivots = jnp.ones((group, k), jnp.float32)
        for j in range(group):
            pivot = jnp.broadcast_to(columns[j][j:j + 1, :], (group, k))
            pivots = jnp.where(sub == j, pivot, pivots)
            if j < group - 1:
                factor = jnp.where(sub > j, columns[j] / pivot, 0.0)
                for m in range(j + 1, group):
                    columns[m] = columns[m] - factor * columns[m][j:j + 1, :]
                left = left - factor * left[j:j + 1, :]
                right = right - factor * right[j:j + 1, :]
        scale = lax.rsqrt(pivots)
        scale = scale * (1.5 - (0.5 * pivots * scale) * scale)
        left = jnp.where(lane >= sub + start, left * scale, 0.0)
        right = right * scale
        upper[start:start + group, :] = left
        inverse[start:start + group, :] = right
        if start + group < k:
            a, b, c = split_three(left)
            x, y, z = split_three(jnp.concatenate([left, right], axis=1))
            work[...] -= lax.dot_general(
                jnp.concatenate([a, a, b, a, b, c], axis=0),
                jnp.concatenate([x, y, x, z, y, x], axis=0),
                (((0,), (0,)), ((), ())), preferred_element_type=jnp.float32,
            )
    factor_ref[...] = upper[...].T * (1.0 / root)
    place = pl.ds(pl.multiple_of(lax.axis_index("col") * width, width), width)
    rows = split(inverse[place, :] * root)
    for r in range(rb):
        block = full_ref[r]
        high = block.astype(jnp.bfloat16)
        low = (block - high.astype(jnp.float32)).astype(jnp.bfloat16)
        ortho_ref[:, r * bs:(r + 1) * bs] = folded(jnp.dot(
            rows, jnp.concatenate([high, low], axis=1), preferred_element_type=jnp.float32
        ))


def factor_and_ortho(root, width, gram, full):
    k = gram.shape[0]
    rb, _, bs = full.shape
    vmem = pl.BlockSpec(memory_space=pltpu.VMEM)
    return pl.pallas_call(
        functools.partial(factor_kernel, root),
        out_shape=(
            jax.ShapeDtypeStruct((width, rb * bs), jnp.float32),
            jax.ShapeDtypeStruct((k, k), jnp.float32),
        ),
        in_specs=[vmem, vmem],
        out_specs=(vmem, vmem),
        scratch_shapes=[
            pltpu.VMEM((k, 2 * k), jnp.float32),
            pltpu.VMEM((k, k), jnp.float32),
            pltpu.VMEM((k, k), jnp.float32),
        ],
        compiler_params=pltpu.CompilerParams(vmem_limit_bytes=24 << 20),
    )(gram, full)


def per_device(start_panel, tile_values, tile_rows, tile_cols, tile_counts):
    position = lax.axis_index("blk")
    n, q = lax.axis_size("blk"), lax.axis_size("col")
    width, vertices = start_panel.shape
    tiles, bs, _ = tile_values.shape
    rb = vertices // bs
    local_cols = (tile_cols // rb - position + REACH + n) % n * rb + tile_cols % rb
    local_rows = tile_rows - position * rb
    live = jnp.arange(tiles, dtype=jnp.int32) < tile_counts[0]
    row_weights = (
        (local_rows[:, None] == jnp.arange(rb, dtype=jnp.int32)[None, :]) & live[:, None]
    ).astype(jnp.float32).reshape(-1)
    full, gram = filtered_and_gram(n, q, start_panel, tile_values, local_cols, row_weights)
    return factor_and_ortho(math.sqrt(vertices * n), width, gram, full)


def solution(mesh):
    in_specs = (P("col", "blk"), P("blk", None, None), P("blk"), P("blk"), P("blk"))
    out_specs = (P("col", "blk"), P())
    return jax.shard_map(
        per_device, mesh=mesh, in_specs=in_specs, out_specs=out_specs, check_vma=False
    )
```
